32 devices in a mesh: rows: 8 (over y, x, core), cols: 4 (over z).
Axes of the slice: x: 2, y: 2, z: 4, core: 2. Of those that a mesh axis runs over, the one named last changes fastest.
Arguments:
- encoded: bfloat16 [256, 128, 384], P('rows', 'cols'), may hold values from -6 to 6
- conv_weight: bfloat16 [3, 3, 384, 384], replicated, may hold values from -0.109375 to 0.109375
- film_table: bfloat16 [360, 2, 384], replicated, may hold values from -3 to 3
- lead: int32 [1], replicated, may hold values from 0 to 359
Outputs:
- updated: bfloat16 [256, 128, 384], P('rows', 'cols')
The draws below stay inside these ranges and needn't reach their ends.
All inputs are finite; a program needn't handle non-finite values.
Results may differ from the reference program's by a relative error of at most 0.006.
Values may be sent and summed in bfloat16 or wider, within the bound.
No kernel may reach another device: no remote copies, remote signals or barrier semaphores. Data moves between devices by JAX's collectives and lax.ppermute only.
A program may use at most 64 MiB of HBM per device.

```python
import jax
import jax.numpy as jnp
from jax import lax

HID = 384
LEADS = 360
DILATION_RATE = 128
NROWS = 256
NCOLS = 128


def block_levels(stream_key, extent, shards, smallest, high):
    def one(axis_at, shards_of):
        heights = jax.random.uniform(jax.random.fold_in(jax.random.fold_in(stream_key, 6), axis_at), (shards_of,), jnp.float32, smallest / len(shards), high / len(shards))
        return jnp.repeat(jnp.exp(heights), extent[axis_at] // shards_of).reshape((-1,) + (1,) * (len(extent) - axis_at - 1))

    loudness = one(*shards[0])
    for cut in shards[1:]:
        loudness = loudness * one(*cut)
    return loudness


def normal_values(rng, shape, width, most, shards=(), held_as=jnp.bfloat16):
    array = jax.random.normal(rng, shape, jnp.float32) * width
    if len(shards) > 0:
        array = block_levels(rng, shape, shards, -0.22, 0.18) * array
    return jnp.clip(array, min=-most, max=most).astype(held_as)


def setup_inputs(seed: int = 0) -> dict:
    arg_keys = jax.random.split(jax.random.key(seed), 5)
    return {
        "encoded": normal_values(arg_keys[0], (NROWS, NCOLS, HID), 1.0, 6.0, ((0, 8), (1, 4))),
        "conv_weight": normal_values(arg_keys[1], (3, 3, HID, HID), (9 * HID) ** -0.5, 0.109375),
        "film_table": normal_values(arg_keys[2], (LEADS, 2, HID), 0.5, 3.0),
        "lead": jax.random.randint(arg_keys[3], (1,), 0, LEADS).astype(jnp.int32),
    }


def reference(encoded, conv_weight, film_table, lead):
    active = jnp.maximum(encoded, jnp.zeros((), jnp.bfloat16))
    conv = lax.conv_general_dilated(
        active.astype(jnp.float32)[None],
        conv_weight.astype(jnp.float32),
        (1, 1),
        [(DILATION_RATE, DILATION_RATE), (DILATION_RATE, DILATION_RATE)],
        rhs_dilation=(DILATION_RATE, DILATION_RATE),
        dimension_numbers=("NHWC", "HWIO", "NHWC"),
        precision=lax.Precision.HIGHEST,
    )[0]
    selected_taps = film_table[lead[0]].astype(jnp.float32)
    updated = encoded.astype(jnp.float32) + conv * (1.0 + selected_taps[0]) + selected_taps[1]
    return updated.astype(jnp.bfloat16)
```

```python
import functools

import jax
import jax.numpy as jnp
from jax import lax
from jax.experimental import pallas as pl
from jax.experimental.pallas import tpu as pltpu
from jax.sharding import PartitionSpec as P

DILATION_RATE = 128
MIB = 1 << 20


def shifted(block, axis, distance):
    devices = range(lax.axis_size(axis))
    route = [(i - distance, i) for i in devices if i - distance in devices]
    return lax.ppermute(block, axis, route)


def relu(block):
    return jnp.maximum(block, jnp.zeros((), block.dtype))


def product(block, tap):
    flat = relu(block).reshape(-1, block.shape[-1])
    return jnp.dot(flat, tap, preferred_element_type=jnp.float32)


def film(film_table, lead):
    chosen = lax.dynamic_index_in_dim(film_table, lead[0], 0, keepdims=False)
    chosen = chosen.astype(jnp.float32)
    return 1.0 + chosen[0], chosen[1]


def any_grid(encoded, conv_weight, film_table, lead, row_step, column_step):
    steps = (-1, 0, 1)
    total = jnp.zeros((encoded.shape[0] * encoded.shape[1], encoded.shape[2]), jnp.float32)
    for ky in steps:
        if abs(ky) * row_step >= lax.axis_size("rows"):
            continue
        strip = shifted(encoded, "rows", -ky * row_step) if ky else encoded
        for kx in steps:
            if abs(kx) * column_step >= lax.axis_size("cols"):
                continue
            block = shifted(strip, "cols", -kx * column_step) if kx else strip
            total = total + product(block, conv_weight[ky + 1, kx + 1])
    scale, beta = film(film_table, lead)
    flat = encoded.reshape(total.shape).astype(jnp.float32)
    return (flat + total * scale + beta).astype(jnp.bfloat16).reshape(encoded.shape)


def finish_kernel(step, other_ref, tap_ref, base_ref, scale_ref, out_ref, stage, sems):
    copies = []
    for k in range(base_ref.shape[0] // step):
        rows = pl.ds(k * step, step)
        active = jnp.maximum(other_ref[rows, :], jnp.zeros((), jnp.bfloat16))
        part = jnp.dot(active, tap_ref[...], preferred_element_type=jnp.float32)
        stage[rows, :] = (base_ref[rows, :] + part * scale_ref[...]).astype(jnp.bfloat16)
        copy = pltpu.make_async_copy(stage.at[rows, :], out_ref.at[rows, :], sems.at[k])
        copy.start()
        copies.append(copy)
    for copy in copies:
        copy.wait()


def finish(other, tap, base, scale):
    cells, chans = base.shape
    step = cells // 4
    whole = pl.BlockSpec(memory_space=pltpu.VMEM)
    return pl.pallas_call(
        functools.partial(finish_kernel, step),
        out_shape=jax.ShapeDtypeStruct(base.shape, jnp.bfloat16),
        in_specs=[whole] * 4,
        out_specs=pl.BlockSpec(memory_space=pl.ANY),
        scratch_shapes=[
            pltpu.VMEM((cells, chans), jnp.bfloat16),
            pltpu.SemaphoreType.DMA((cells // step,)),
        ],
        compiler_params=pltpu.CompilerParams(vmem_limit_bytes=16 * MIB),
        cost_estimate=pl.CostEstimate(
            flops=2 * cells * chans * chans,
            bytes_accessed=10 * cells * chans,
            transcendentals=0,
        ),
    )(other, tap, base, scale)


def paired(encoded, conv_weight, film_table, lead, row_step):
    count = lax.axis_size("rows")
    other = lax.ppermute(encoded, "rows", [(i, (i + row_step) % count) for i in range(count)])
    above = lax.axis_index("rows") < row_step
    column = conv_weight[:, 1]
    far_tap = lax.dynamic_index_in_dim(column, jnp.where(above, 2, 0), 0, keepdims=False)
    scale, beta = film(film_table, lead)
    near = product(encoded, column[1])
    base = encoded.reshape(near.shape).astype(jnp.float32) + near * scale + beta
    updated = finish(other.reshape(near.shape), far_tap, base, scale[None])
    return updated.reshape(encoded.shape)


def local(encoded, conv_weight, film_table, lead):
    row_step = DILATION_RATE // encoded.shape[0]
    column_step = DILATION_RATE // encoded.shape[1]
    if lax.axis_size("rows") == 2 * row_step and column_step >= lax.axis_size("cols"):
        return paired(encoded, conv_weight, film_table, lead, row_step)
    return any_grid(encoded, conv_weight, film_table, lead, row_step, column_step)


def solution(mesh):
    placed = (P("rows", "cols", None), P(), P(), P())
    return jax.shard_map(
        local, mesh=mesh, in_specs=placed, out_specs=P("rows", "cols", None), check_vma=False
    )
```

```python
import functools

import jax
import jax.numpy as jnp
from jax import lax
from jax.experimental import pallas as pl
from jax.experimental.pallas import tpu as pltpu
from jax.sharding import PartitionSpec as P

DILATION_RATE = 128
MIB = 1 << 20


def shifted(block, axis, distance):
    devices = range(lax.axis_size(axis))
    route = [(i - distance, i) for i in devices if i - distance in devices]
    return lax.ppermute(block, axis, route)


def relu(block):
    return jnp.maximum(block, jnp.zeros((), block.dtype))


def product(block, tap):
    flat = relu(block).reshape(-1, block.shape[-1])
    return jnp.dot(flat, tap, preferred_element_type=jnp.float32)


def film(film_table, lead):
    chosen = lax.dynamic_index_in_dim(film_table, lead[0], 0, keepdims=False)
    chosen = chosen.astype(jnp.float32)
    return 1.0 + chosen[0], chosen[1]


def any_grid(encoded, conv_weight, film_table, lead, row_step, column_step):
    steps = (-1, 0, 1)
    total = jnp.zeros((encoded.shape[0] * encoded.shape[1], encoded.shape[2]), jnp.float32)
    for ky in steps:
        if abs(ky) * row_step >= lax.axis_size("rows"):
            continue
        strip = shifted(encoded, "rows", -ky * row_step) if ky else encoded
        for kx in steps:
            if abs(kx) * column_step >= lax.axis_size("cols"):
                continue
            block = shifted(strip, "cols", -kx * column_step) if kx else strip
            total = total + product(block, conv_weight[ky + 1, kx + 1])
    scale, beta = film(film_table, lead)
    flat = encoded.reshape(total.shape).astype(jnp.float32)
    return (flat + total * scale + beta).astype(jnp.bfloat16).reshape(encoded.shape)


def finish_kernel(cuts, other_ref, tap_ref, base_ref, scale_ref, out_ref, stage, sems):
    copies = []
    for k, (start, stop) in enumerate(zip(cuts[:-1], cuts[1:])):
        rows = pl.ds(start, stop - start)
        active = jnp.maximum(other_ref[rows, :], jnp.zeros((), jnp.bfloat16))
        part = jnp.dot(active, tap_ref[...], preferred_element_type=jnp.float32)
        stage[rows, :] = (base_ref[rows, :] + part * scale_ref[...]).astype(jnp.bfloat16)
        copy = pltpu.make_async_copy(stage.at[rows, :], out_ref.at[rows, :], sems.at[k])
        copy.start()
        copies.append(copy)
    for copy in copies:
        copy.wait()


def finish(other, tap, base, scale):
    cells, chans = base.shape
    cuts = [cells * eighth // 8 for eighth in (0, 2, 4, 6, 7, 8)]
    whole = pl.BlockSpec(memory_space=pltpu.VMEM)
    return pl.pallas_call(
        functools.partial(finish_kernel, cuts),
        out_shape=jax.ShapeDtypeStruct(base.shape, jnp.bfloat16),
        in_specs=[whole] * 4,
        out_specs=pl.BlockSpec(memory_space=pl.ANY),
        scratch_shapes=[
            pltpu.VMEM((cells, chans), jnp.bfloat16),
            pltpu.SemaphoreType.DMA((len(cuts) - 1,)),
        ],
        compiler_params=pltpu.CompilerParams(vmem_limit_bytes=16 * MIB),
        cost_estimate=pl.CostEstimate(
            flops=2 * cells * chans * chans,
            bytes_accessed=10 * cells * chans,
            transcendentals=0,
        ),
    )(other, tap, base, scale)


def paired(encoded, conv_weight, film_table, lead, row_step):
    count = lax.axis_size("rows")
    other = lax.ppermute(encoded, "rows", [(i, (i + row_step) % count) for i in range(count)])
    above = lax.axis_index("rows") < row_step
    column = conv_weight[:, 1]
    far_tap = lax.dynamic_index_in_dim(column, jnp.where(above, 2, 0), 0, keepdims=False)
    scale, beta = film(film_table, lead)
    near = product(encoded, column[1])
    base = encoded.reshape(near.shape).astype(jnp.float32) + near * scale + beta
    updated = finish(other.reshape(near.shape), far_tap, base, scale[None])
    return updated.reshape(encoded.shape)


def local(encoded, conv_weight, film_table, lead):
    row_step = DILATION_RATE // encoded.shape[0]
    column_step = DILATION_RATE // encoded.shape[1]
    if lax.axis_size("rows") == 2 * row_step and column_step >= lax.axis_size("cols"):
        return paired(encoded, conv_weight, film_table, lead, row_step)
    return any_grid(encoded, conv_weight, film_table, lead, row_step, column_step)


def solution(mesh):
    placed = (P("rows", "cols", None), P(), P(), P())
    return jax.shard_map(
        local, mesh=mesh, in_specs=placed, out_specs=P("rows", "cols", None), check_vma=False
    )
```

```python
import functools

import jax
import jax.numpy as jnp
from jax import lax
from jax.experimental import pallas as pl
from jax.experimental.pallas import tpu as pltpu
from jax.sharding import PartitionSpec as P

DILATION_RATE = 128
MIB = 1 << 20


def shifted(block, axis, distance):
    devices = range(lax.axis_size(axis))
    route = [(i - distance, i) for i in devices if i - distance in devices]
    return lax.ppermute(block, axis, route)


def relu(block):
    return jnp.maximum(block, jnp.zeros((), block.dtype))


def product(block, tap):
    flat = relu(block).reshape(-1, block.shape[-1])
    return jnp.dot(flat, tap, preferred_element_type=jnp.float32)


def film(film_table, lead):
    chosen = lax.dynamic_index_in_dim(film_table, lead[0], 0, keepdims=False)
    chosen = chosen.astype(jnp.float32)
    return 1.0 + chosen[0], chosen[1]


def any_grid(encoded, conv_weight, film_table, lead, row_step, column_step):
    steps = (-1, 0, 1)
    total = jnp.zeros((encoded.shape[0] * encoded.shape[1], encoded.shape[2]), jnp.float32)
    for ky in steps:
        if abs(ky) * row_step >= lax.axis_size("rows"):
            continue
        strip = shifted(encoded, "rows", -ky * row_step) if ky else encoded
        for kx in steps:
            if abs(kx) * column_step >= lax.axis_size("cols"):
                continue
            block = shifted(strip, "cols", -kx * column_step) if kx else strip
            total = total + product(block, conv_weight[ky + 1, kx + 1])
    scale, beta = film(film_table, lead)
    flat = encoded.reshape(total.shape).astype(jnp.float32)
    return (flat + total * scale + beta).astype(jnp.bfloat16).reshape(encoded.shape)


def finish_kernel(cuts, other_ref, tap_ref, base_ref, scale_ref, out_ref, stage, sems):
    copies = []
    for k, (start, stop) in enumerate(zip(cuts[:-1], cuts[1:])):
        rows = pl.ds(start, stop - start)
        active = jnp.maximum(other_ref[rows, :], jnp.zeros((), jnp.bfloat16))
        part = jnp.dot(active, tap_ref[...], preferred_element_type=jnp.float32)
        stage[rows, :] = (base_ref[rows, :] + part * scale_ref[...]).astype(jnp.bfloat16)
        copy = pltpu.make_async_copy(stage.at[rows, :], out_ref.at[rows, :], sems.at[k])
        copy.start()
        copies.append(copy)
    for copy in copies:
        copy.wait()


def finish(other, tap, base, scale):
    cells, chans = base.shape
    cuts = [cells * eighth // 8 for eighth in (0, 1, 2, 4, 6, 7, 8)]
    whole = pl.BlockSpec(memory_space=pltpu.VMEM)
    return pl.pallas_call(
        functools.partial(finish_kernel, cuts),
        out_shape=jax.ShapeDtypeStruct(base.shape, jnp.bfloat16),
        in_specs=[whole] * 4,
        out_specs=pl.BlockSpec(memory_space=pl.ANY),
        scratch_shapes=[
            pltpu.VMEM((cells, chans), jnp.bfloat16),
            pltpu.SemaphoreType.DMA((len(cuts) - 1,)),
        ],
        compiler_params=pltpu.CompilerParams(vmem_limit_bytes=16 * MIB),
        cost_estimate=pl.CostEstimate(
            flops=2 * cells * chans * chans,
            bytes_accessed=10 * cells * chans,
            transcendentals=0,
        ),
    )(other, tap, base, scale)


def paired(encoded, conv_weight, film_table, lead, row_step):
    count = lax.axis_size("rows")
    other = lax.ppermute(encoded, "rows", [(i, (i + row_step) % count) for i in range(count)])
    above = lax.axis_index("rows") < row_step
    column = conv_weight[:, 1]
    far_tap = lax.dynamic_index_in_dim(column, jnp.where(above, 2, 0), 0, keepdims=False)
    scale, beta = film(film_table, lead)
    near = product(encoded, column[1])
    base = encoded.reshape(near.shape).astype(jnp.float32) + near * scale + beta
    updated = finish(other.reshape(near.shape), far_tap, base, scale[None])
    return updated.reshape(encoded.shape)


def local(encoded, conv_weight, film_table, lead):
    row_step = DILATION_RATE // encoded.shape[0]
    column_step = DILATION_RATE // encoded.shape[1]
    if lax.axis_size("rows") == 2 * row_step and column_step >= lax.axis_size("cols"):
        return paired(encoded, conv_weight, film_table, lead, row_step)
    return any_grid(encoded, conv_weight, film_table, lead, row_step, column_step)


def solution(mesh):
    placed = (P("rows", "cols", None), P(), P(), P())
    return jax.shard_map(
        local, mesh=mesh, in_specs=placed, out_specs=P("rows", "cols", None), check_vma=False
    )
```

```python
import functools

import jax
import jax.numpy as jnp
from jax import lax
from jax.experimental import pallas as pl
from jax.experimental.pallas import tpu as pltpu
from jax.sharding import PartitionSpec as P

DILATION_RATE = 128
MIB = 1 << 20


def shifted(block, axis, distance):
    devices = range(lax.axis_size(axis))
    route = [(i - distance, i) for i in devices if i - distance in devices]
    return lax.ppermute(block, axis, route)


def relu(block):
    return jnp.maximum(block, jnp.zeros((), block.dtype))


def product(block, tap):
    flat = relu(block).reshape(-1, block.shape[-1])
    return jnp.dot(flat, tap, preferred_element_type=jnp.float32)


def film(film_table, lead):
    chosen = lax.dynamic_index_in_dim(film_table, lead[0], 0, keepdims=False)
    chosen = chosen.astype(jnp.float32)
    return 1.0 + chosen[0], chosen[1]


def any_grid(encoded, conv_weight, film_table, lead, row_step, column_step):
    steps = (-1, 0, 1)
    total = jnp.zeros((encoded.shape[0] * encoded.shape[1], encoded.shape[2]), jnp.float32)
    for ky in steps:
        if abs(ky) * row_step >= lax.axis_size("rows"):
            continue
        strip = shifted(encoded, "rows", -ky * row_step) if ky else encoded
        for kx in steps:
            if abs(kx) * column_step >= lax.axis_size("cols"):
                continue
            block = shifted(strip, "cols", -kx * column_step) if kx else strip
            total = total + product(block, conv_weight[ky + 1, kx + 1])
    scale, beta = film(film_table, lead)
    flat = encoded.reshape(total.shape).astype(jnp.float32)
    return (flat + total * scale + beta).astype(jnp.bfloat16).reshape(encoded.shape)


def finish_kernel(cuts, other_ref, tap_ref, base_ref, scale_ref, out_ref, stage, sems):
    copies = []
    for k, (start, stop) in enumerate(zip(cuts[:-1], cuts[1:])):
        rows = pl.ds(start, stop - start)
        active = jnp.maximum(other_ref[rows, :], jnp.zeros((), jnp.bfloat16))
        part = jnp.dot(active, tap_ref[...], preferred_element_type=jnp.float32)
        stage[rows, :] = (base_ref[rows, :] + part * scale_ref[...]).astype(jnp.bfloat16)
        copy = pltpu.make_async_copy(stage.at[rows, :], out_ref.at[rows, :], sems.at[k])
        copy.start()
        copies.append(copy)
    for copy in copies:
        copy.wait()


def finish(other, tap, base, scale):
    cells, chans = base.shape
    cuts = [cells * eighth // 8 for eighth in (0, 4, 6, 7, 8)]
    whole = pl.BlockSpec(memory_space=pltpu.VMEM)
    return pl.pallas_call(
        functools.partial(finish_kernel, cuts),
        out_shape=jax.ShapeDtypeStruct(base.shape, jnp.bfloat16),
        in_specs=[whole] * 4,
        out_specs=pl.BlockSpec(memory_space=pl.ANY),
        scratch_shapes=[
            pltpu.VMEM((cells, chans), jnp.bfloat16),
            pltpu.SemaphoreType.DMA((len(cuts) - 1,)),
        ],
        compiler_params=pltpu.CompilerParams(vmem_limit_bytes=16 * MIB),
        cost_estimate=pl.CostEstimate(
            flops=2 * cells * chans * chans,
            bytes_accessed=10 * cells * chans,
            transcendentals=0,
        ),
    )(other, tap, base, scale)


def paired(encoded, conv_weight, film_table, lead, row_step):
    count = lax.axis_size("rows")
    other = lax.ppermute(encoded, "rows", [(i, (i + row_step) % count) for i in range(count)])
    above = lax.axis_index("rows") < row_step
    column = conv_weight[:, 1]
    far_tap = lax.dynamic_index_in_dim(column, jnp.where(above, 2, 0), 0, keepdims=False)
    scale, beta = film(film_table, lead)
    near = product(encoded, column[1])
    base = encoded.reshape(near.shape).astype(jnp.float32) + near * scale + beta
    updated = finish(other.reshape(near.shape), far_tap, base, scale[None])
    return updated.reshape(encoded.shape)


def local(encoded, conv_weight, film_table, lead):
    row_step = DILATION_RATE // encoded.shape[0]
    column_step = DILATION_RATE // encoded.shape[1]
    if lax.axis_size("rows") == 2 * row_step and column_step >= lax.axis_size("cols"):
        return paired(encoded, conv_weight, film_table, lead, row_step)
    return any_grid(encoded, conv_weight, film_table, lead, row_step, column_step)


def solution(mesh):
    placed = (P("rows", "cols", None), P(), P(), P())
    return jax.shard_map(
        local, mesh=mesh, in_specs=placed, out_specs=P("rows", "cols", None), check_vma=False
    )
```

```python
import functools

import jax
import jax.numpy as jnp
from jax import lax
from jax.experimental import pallas as pl
from jax.experimental.pallas import tpu as pltpu
from jax.sharding import PartitionSpec as P

DILATION_RATE = 128
MIB = 1 << 20


def shifted(block, axis, distance):
    devices = range(lax.axis_size(axis))
    route = [(i - distance, i) for i in devices if i - distance in devices]
    return lax.ppermute(block, axis, route)


def relu(block):
    return jnp.maximum(block, jnp.zeros((), block.dtype))


def product(block, tap):
    flat = relu(block).reshape(-1, block.shape[-1])
    return jnp.dot(flat, tap, preferred_element_type=jnp.float32)


def film(film_table, lead):
    chosen = lax.dynamic_index_in_dim(film_table, lead[0], 0, keepdims=False)
    chosen = chosen.astype(jnp.float32)
    return 1.0 + chosen[0], chosen[1]


def any_grid(encoded, conv_weight, film_table, lead, row_step, column_step):
    steps = (-1, 0, 1)
    total = jnp.zeros((encoded.shape[0] * encoded.shape[1], encoded.shape[2]), jnp.float32)
    for ky in steps:
        if abs(ky) * row_step >= lax.axis_size("rows"):
            continue
        strip = shifted(encoded, "rows", -ky * row_step) if ky else encoded
        for kx in steps:
            if abs(kx) * column_step >= lax.axis_size("cols"):
                continue
            block = shifted(strip, "cols", -kx * column_step) if kx else strip
            total = total + product(block, conv_weight[ky + 1, kx + 1])
    scale, beta = film(film_table, lead)
    flat = encoded.reshape(total.shape).astype(jnp.float32)
    return (flat + total * scale + beta).astype(jnp.bfloat16).reshape(encoded.shape)


def finish_kernel(
    cuts, other_ref, tap_ref, twin_ref, base_ref, scale_ref, out_ref, stage, sems
):
    deep = tap_ref.shape[0]
    wide = other_ref.shape[1] - deep
    copies = []
    for k, (start, stop) in enumerate(zip(cuts[:-1], cuts[1:])):
        rows = pl.ds(start, stop - start)
        active = jnp.maximum(other_ref[rows, :], jnp.zeros((), jnp.bfloat16))
        part = jnp.dot(active[:, :deep], tap_ref[...], preferred_element_type=jnp.float32)
        count = (stop - start) // 2
        twins = jnp.concatenate([active[:count, deep:], active[count:, deep:]], axis=1)
        rest = jnp.dot(twins, twin_ref[...], preferred_element_type=jnp.float32)
        halves = [
            jnp.concatenate(
                [rest[:, k : k + wide] for k in range(side * wide, rest.shape[1], 2 * wide)], axis=1
            )
            for side in range(2)
        ]
        part = part + jnp.concatenate(halves, axis=0)
        stage[rows, :] = (base_ref[rows, :] + part * scale_ref[...]).astype(jnp.bfloat16)
        copy = pltpu.make_async_copy(stage.at[rows, :], out_ref.at[rows, :], sems.at[k])
        copy.start()
        copies.append(copy)
    for copy in copies:
        copy.wait()


def twin_tap(tap, wide):
    parts = []
    for k in range(0, tap.shape[1], wide):
        part = tap[:, k : k + wide]
        empty = jnp.zeros_like(part)
        parts += [jnp.concatenate([part, empty]), jnp.concatenate([empty, part])]
    return jnp.concatenate(parts, axis=1)


def finish(other, tap, base, scale):
    cells, chans = base.shape
    deep = chans * 2 // 3
    tap, twin = tap[:deep], twin_tap(tap[deep:], chans - deep)
    cuts = [cells * eighth // 8 for eighth in (0, 2, 4, 6, 8)]
    whole = pl.BlockSpec(memory_space=pltpu.VMEM)
    return pl.pallas_call(
        functools.partial(finish_kernel, cuts),
        out_shape=jax.ShapeDtypeStruct(base.shape, jnp.bfloat16),
        in_specs=[whole] * 5,
        out_specs=pl.BlockSpec(memory_space=pl.ANY),
        scratch_shapes=[
            pltpu.VMEM((cells, chans), jnp.bfloat16),
            pltpu.SemaphoreType.DMA((len(cuts) - 1,)),
        ],
        compiler_params=pltpu.CompilerParams(vmem_limit_bytes=16 * MIB),
        cost_estimate=pl.CostEstimate(
            flops=2 * cells * chans * chans,
            bytes_accessed=10 * cells * chans,
            transcendentals=0,
        ),
    )(other, tap, twin, base, scale)


def paired(encoded, conv_weight, film_table, lead, row_step):
    count = lax.axis_size("rows")
    other = lax.ppermute(encoded, "rows", [(i, (i + row_step) % count) for i in range(count)])
    above = lax.axis_index("rows") < row_step
    column = conv_weight[:, 1]
    far_tap = lax.dynamic_index_in_dim(column, jnp.where(above, 2, 0), 0, keepdims=False)
    scale, beta = film(film_table, lead)
    near = product(encoded, column[1])
    base = encoded.reshape(near.shape).astype(jnp.float32) + near * scale + beta
    updated = finish(other.reshape(near.shape), far_tap, base, scale[None])
    return updated.reshape(encoded.shape)


def local(encoded, conv_weight, film_table, lead):
    row_step = DILATION_RATE // encoded.shape[0]
    column_step = DILATION_RATE // encoded.shape[1]
    if lax.axis_size("rows") == 2 * row_step and column_step >= lax.axis_size("cols"):
        return paired(encoded, conv_weight, film_table, lead, row_step)
    return any_grid(encoded, conv_weight, film_table, lead, row_step, column_step)


def solution(mesh):
    placed = (P("rows", "cols", None), P(), P(), P())
    return jax.shard_map(
        local, mesh=mesh, in_specs=placed, out_specs=P("rows", "cols", None), check_vma=False
    )
```

```python
import functools

import jax
import jax.numpy as jnp
from jax import lax
from jax.experimental import pallas as pl
from jax.experimental.pallas import tpu as pltpu
from jax.sharding import PartitionSpec as P

DILATION_RATE = 128
MIB = 1 << 20


def shifted(block, axis, distance):
    devices = range(lax.axis_size(axis))
    route = [(i - distance, i) for i in devices if i - distance in devices]
    return lax.ppermute(block, axis, route)


def relu(block):
    return jnp.maximum(block, jnp.zeros((), block.dtype))


def product(block, tap):
    flat = relu(block).reshape(-1, block.shape[-1])
    return jnp.dot(flat, tap, preferred_element_type=jnp.float32)


def film(film_table, lead):
    chosen = lax.dynamic_index_in_dim(film_table, lead[0], 0, keepdims=False)
    chosen = chosen.astype(jnp.float32)
    return 1.0 + chosen[0], chosen[1]


def any_grid(encoded, conv_weight, film_table, lead, row_step, column_step):
    steps = (-1, 0, 1)
    total = jnp.zeros((encoded.shape[0] * encoded.shape[1], encoded.shape[2]), jnp.float32)
    for ky in steps:
        if abs(ky) * row_step >= lax.axis_size("rows"):
            continue
        strip = shifted(encoded, "rows", -ky * row_step) if ky else encoded
        for kx in steps:
            if abs(kx) * column_step >= lax.axis_size("cols"):
                continue
            block = shifted(strip, "cols", -kx * column_step) if kx else strip
            total = total + product(block, conv_weight[ky + 1, kx + 1])
    scale, beta = film(film_table, lead)
    flat = encoded.reshape(total.shape).astype(jnp.float32)
    return (flat + total * scale + beta).astype(jnp.bfloat16).reshape(encoded.shape)


def finish_kernel(cuts, other_ref, tap_ref, base_ref, scale_ref, out_ref, stage, sems):
    spans = list(zip(cuts[:-1], cuts[1:]))
    copies = []
    for k, (start, stop) in enumerate(spans):
        rows = pl.ds(start, stop - start)
        active = jnp.maximum(other_ref[rows, :], jnp.zeros((), jnp.bfloat16))
        part = jnp.dot(active, tap_ref[...], preferred_element_type=jnp.float32)
        stage[rows, :] = (base_ref[rows, :] + part * scale_ref[...]).astype(jnp.bfloat16)
        copies.append(pltpu.make_async_copy(stage.at[rows, :], out_ref.at[rows, :], sems.at[k]))
        if k:
            copies[k - 1].start()
    copies[-1].start()
    for copy in copies:
        copy.wait()


def finish(other, tap, base, scale):
    cells, chans = base.shape
    cuts = [cells * eighth // 8 for eighth in (0, 1, 3, 5, 7, 8)]
    whole = pl.BlockSpec(memory_space=pltpu.VMEM)
    return pl.pallas_call(
        functools.partial(finish_kernel, cuts),
        out_shape=jax.ShapeDtypeStruct(base.shape, jnp.bfloat16),
        in_specs=[whole] * 4,
        out_specs=pl.BlockSpec(memory_space=pl.ANY),
        scratch_shapes=[
            pltpu.VMEM((cells, chans), jnp.bfloat16),
            pltpu.SemaphoreType.DMA((len(cuts) - 1,)),
        ],
        compiler_params=pltpu.CompilerParams(vmem_limit_bytes=16 * MIB),
        cost_estimate=pl.CostEstimate(
            flops=2 * cells * chans * chans,
            bytes_accessed=10 * cells * chans,
            transcendentals=0,
        ),
    )(other, tap, base, scale)


def paired(encoded, conv_weight, film_table, lead, row_step):
    count = lax.axis_size("rows")
    other = lax.ppermute(encoded, "rows", [(i, (i + row_step) % count) for i in range(count)])
    above = lax.axis_index("rows") < row_step
    column = conv_weight[:, 1]
    far_tap = lax.dynamic_index_in_dim(column, jnp.where(above, 2, 0), 0, keepdims=False)
    scale, beta = film(film_table, lead)
    near = product(encoded, column[1])
    base = encoded.reshape(near.shape).astype(jnp.float32) + near * scale + beta
    updated = finish(other.reshape(near.shape), far_tap, base, scale[None])
    return updated.reshape(encoded.shape)


def local(encoded, conv_weight, film_table, lead):
    row_step = DILATION_RATE // encoded.shape[0]
    column_step = DILATION_RATE // encoded.shape[1]
    if lax.axis_size("rows") == 2 * row_step and column_step >= lax.axis_size("cols"):
        return paired(encoded, conv_weight, film_table, lead, row_step)
    return any_grid(encoded, conv_weight, film_table, lead, row_step, column_step)


def solution(mesh):
    placed = (P("rows", "cols", None), P(), P(), P())
    return jax.shard_map(
        local, mesh=mesh, in_specs=placed, out_specs=P("rows", "cols", None), check_vma=False
    )
```

```python
import functools

import jax
import jax.numpy as jnp
from jax import lax
from jax.experimental import pallas as pl
from jax.experimental.pallas import tpu as pltpu
from jax.sharding import PartitionSpec as P

DILATION_RATE = 128
MIB = 1 << 20


def shifted(block, axis, distance):
    devices = range(lax.axis_size(axis))
    route = [(i - distance, i) for i in devices if i - distance in devices]
    return lax.ppermute(block, axis, route)


def relu(block):
    return jnp.maximum(block, jnp.zeros((), block.dtype))


def product(block, tap):
    flat = relu(block).reshape(-1, block.shape[-1])
    return jnp.dot(flat, tap, preferred_element_type=jnp.float32)


def film(film_table, lead):
    chosen = lax.dynamic_index_in_dim(film_table, lead[0], 0, keepdims=False)
    chosen = chosen.astype(jnp.float32)
    return 1.0 + chosen[0], chosen[1]


def any_grid(encoded, conv_weight, film_table, lead, row_step, column_step):
    steps = (-1, 0, 1)
    total = jnp.zeros((encoded.shape[0] * encoded.shape[1], encoded.shape[2]), jnp.float32)
    for ky in steps:
        if abs(ky) * row_step >= lax.axis_size("rows"):
            continue
        strip = shifted(encoded, "rows", -ky * row_step) if ky else encoded
        for kx in steps:
            if abs(kx) * column_step >= lax.axis_size("cols"):
                continue
            block = shifted(strip, "cols", -kx * column_step) if kx else strip
            total = total + product(block, conv_weight[ky + 1, kx + 1])
    scale, beta = film(film_table, lead)
    flat = encoded.reshape(total.shape).astype(jnp.float32)
    return (flat + total * scale + beta).astype(jnp.bfloat16).reshape(encoded.shape)


def finish_kernel(cuts, other_ref, tap_ref, base_ref, scale_ref, out_ref, stage, sems):
    copies = []
    for k, (start, stop) in enumerate(zip(cuts[:-1], cuts[1:])):
        rows = pl.ds(start, stop - start)
        active = jnp.maximum(other_ref[rows, :], jnp.zeros((), jnp.bfloat16))
        part = jnp.dot(active, tap_ref[...], preferred_element_type=jnp.float32)
        stage[rows, :] = (base_ref[rows, :] + part * scale_ref[...]).astype(jnp.bfloat16)
        copy = pltpu.make_async_copy(stage.at[rows, :], out_ref.at[rows, :], sems.at[k])
        copy.start()
        copies.append(copy)
    for copy in copies:
        copy.wait()


def finish(other, tap, base, scale):
    cells, chans = base.shape
    cuts = [cells * part // 16 for part in (0, 4, 8, 12, 14, 15, 16)]
    whole = pl.BlockSpec(memory_space=pltpu.VMEM)
    return pl.pallas_call(
        functools.partial(finish_kernel, cuts),
        out_shape=jax.ShapeDtypeStruct(base.shape, jnp.bfloat16),
        in_specs=[whole] * 4,
        out_specs=pl.BlockSpec(memory_space=pl.ANY),
        scratch_shapes=[
            pltpu.VMEM((cells, chans), jnp.bfloat16),
            pltpu.SemaphoreType.DMA((len(cuts) - 1,)),
        ],
        compiler_params=pltpu.CompilerParams(vmem_limit_bytes=16 * MIB),
        cost_estimate=pl.CostEstimate(
            flops=2 * cells * chans * chans,
            bytes_accessed=10 * cells * chans,
            transcendentals=0,
        ),
    )(other, tap, base, scale)


def paired(encoded, conv_weight, film_table, lead, row_step):
    count = lax.axis_size("rows")
    other = lax.ppermute(encoded, "rows", [(i, (i + row_step) % count) for i in range(count)])
    above = lax.axis_index("rows") < row_step
    column = conv_weight[:, 1]
    far_tap = lax.dynamic_index_in_dim(column, jnp.where(above, 2, 0), 0, keepdims=False)
    scale, beta = film(film_table, lead)
    near = product(encoded, column[1])
    base = encoded.reshape(near.shape).astype(jnp.float32) + near * scale + beta
    updated = finish(other.reshape(near.shape), far_tap, base, scale[None])
    return updated.reshape(encoded.shape)


def local(encoded, conv_weight, film_table, lead):
    row_step = DILATION_RATE // encoded.shape[0]
    column_step = DILATION_RATE // encoded.shape[1]
    if lax.axis_size("rows") == 2 * row_step and column_step >= lax.axis_size("cols"):
        return paired(encoded, conv_weight, film_table, lead, row_step)
    return any_grid(encoded, conv_weight, film_table, lead, row_step, column_step)


def solution(mesh):
    placed = (P("rows", "cols", None), P(), P(), P())
    return jax.shard_map(
        local, mesh=mesh, in_specs=placed, out_specs=P("rows", "cols", None), check_vma=False
    )
```

```python
import functools

import jax
import jax.numpy as jnp
from jax import lax
from jax.experimental import pallas as pl
from jax.experimental.pallas import tpu as pltpu
from jax.sharding import PartitionSpec as P

DILATION_RATE = 128
MIB = 1 << 20


def shifted(block, axis, distance):
    devices = range(lax.axis_size(axis))
    route = [(i - distance, i) for i in devices if i - distance in devices]
    return lax.ppermute(block, axis, route)


def relu(block):
    return jnp.maximum(block, jnp.zeros((), block.dtype))


def product(block, tap):
    flat = relu(block).reshape(-1, block.shape[-1])
    return jnp.dot(flat, tap, preferred_element_type=jnp.float32)


def film(film_table, lead):
    chosen = lax.dynamic_index_in_dim(film_table, lead[0], 0, keepdims=False)
    chosen = chosen.astype(jnp.float32)
    return 1.0 + chosen[0], chosen[1]


def any_grid(encoded, conv_weight, film_table, lead, row_step, column_step):
    steps = (-1, 0, 1)
    total = jnp.zeros((encoded.shape[0] * encoded.shape[1], encoded.shape[2]), jnp.float32)
    for ky in steps:
        if abs(ky) * row_step >= lax.axis_size("rows"):
            continue
        strip = shifted(encoded, "rows", -ky * row_step) if ky else encoded
        for kx in steps:
            if abs(kx) * column_step >= lax.axis_size("cols"):
                continue
            block = shifted(strip, "cols", -kx * column_step) if kx else strip
            total = total + product(block, conv_weight[ky + 1, kx + 1])
    scale, beta = film(film_table, lead)
    flat = encoded.reshape(total.shape).astype(jnp.float32)
    return (flat + total * scale + beta).astype(jnp.bfloat16).reshape(encoded.shape)


def finish_kernel(cuts, other_ref, tap_ref, base_ref, scale_ref, out_ref, stage, sem):
    for start, stop in zip(cuts[:-1], cuts[1:]):
        rows = pl.ds(start, stop - start)
        active = jnp.maximum(other_ref[rows, :], jnp.zeros((), jnp.bfloat16))
        part = jnp.dot(active, tap_ref[...], preferred_element_type=jnp.float32)
        stage[rows, :] = (base_ref[rows, :] + part * scale_ref[...]).astype(jnp.bfloat16)
        pltpu.make_async_copy(stage.at[rows, :], out_ref.at[rows, :], sem).start()
    pltpu.make_async_copy(stage, out_ref, sem).wait()


def finish(other, tap, base, scale):
    cells, chans = base.shape
    cuts = [cells * part // 16 for part in (0, 4, 8, 12, 14, 15, 16)]
    whole = pl.BlockSpec(memory_space=pltpu.VMEM)
    return pl.pallas_call(
        functools.partial(finish_kernel, cuts),
        out_shape=jax.ShapeDtypeStruct(base.shape, jnp.bfloat16),
        in_specs=[whole] * 4,
        out_specs=pl.BlockSpec(memory_space=pl.ANY),
        scratch_shapes=[
            pltpu.VMEM((cells, chans), jnp.bfloat16),
            pltpu.SemaphoreType.DMA,
        ],
        compiler_params=pltpu.CompilerParams(vmem_limit_bytes=16 * MIB),
        cost_estimate=pl.CostEstimate(
            flops=2 * cells * chans * chans,
            bytes_accessed=10 * cells * chans,
            transcendentals=0,
        ),
    )(other, tap, base, scale)


def paired(encoded, conv_weight, film_table, lead, row_step):
    count = lax.axis_size("rows")
    other = lax.ppermute(encoded, "rows", [(i, (i + row_step) % count) for i in range(count)])
    above = lax.axis_index("rows") < row_step
    column = conv_weight[:, 1]
    far_tap = lax.dynamic_index_in_dim(column, jnp.where(above, 2, 0), 0, keepdims=False)
    scale, beta = film(film_table, lead)
    near = product(encoded, column[1])
    base = encoded.reshape(near.shape).astype(jnp.float32) + near * scale + beta
    updated = finish(other.reshape(near.shape), far_tap, base, scale[None])
    return updated.reshape(encoded.shape)


def local(encoded, conv_weight, film_table, lead):
    row_step = DILATION_RATE // encoded.shape[0]
    column_step = DILATION_RATE // encoded.shape[1]
    if lax.axis_size("rows") == 2 * row_step and column_step >= lax.axis_size("cols"):
        return paired(encoded, conv_weight, film_table, lead, row_step)
    return any_grid(encoded, conv_weight, film_table, lead, row_step, column_step)


def solution(mesh):
    placed = (P("rows", "cols", None), P(), P(), P())
    return jax.shard_map(
        local, mesh=mesh, in_specs=placed, out_specs=P("rows", "cols", None), check_vma=False
    )
```

```python
import functools

import jax
import jax.numpy as jnp
from jax import lax
from jax.experimental import pallas as pl
from jax.experimental.pallas import tpu as pltpu
from jax.sharding import PartitionSpec as P

DILATION_RATE = 128
MIB = 1 << 20


def shifted(block, axis, distance):
    devices = range(lax.axis_size(axis))
    route = [(i - distance, i) for i in devices if i - distance in devices]
    return lax.ppermute(block, axis, route)


def relu(block):
    return jnp.maximum(block, jnp.zeros((), block.dtype))


def product(block, tap):
    flat = relu(block).reshape(-1, block.shape[-1])
    return jnp.dot(flat, tap, preferred_element_type=jnp.float32)


def film(film_table, lead):
    chosen = lax.dynamic_index_in_dim(film_table, lead[0], 0, keepdims=False)
    chosen = chosen.astype(jnp.float32)
    return 1.0 + chosen[0], chosen[1]


def any_grid(encoded, conv_weight, film_table, lead, row_step, column_step):
    steps = (-1, 0, 1)
    total = jnp.zeros((encoded.shape[0] * encoded.shape[1], encoded.shape[2]), jnp.float32)
    for ky in steps:
        if abs(ky) * row_step >= lax.axis_size("rows"):
            continue
        strip = shifted(encoded, "rows", -ky * row_step) if ky else encoded
        for kx in steps:
            if abs(kx) * column_step >= lax.axis_size("cols"):
                continue
            block = shifted(strip, "cols", -kx * column_step) if kx else strip
            total = total + product(block, conv_weight[ky + 1, kx + 1])
    scale, beta = film(film_table, lead)
    flat = encoded.reshape(total.shape).astype(jnp.float32)
    return (flat + total * scale + beta).astype(jnp.bfloat16).reshape(encoded.shape)


def finish_kernel(cuts, other_ref, tap_ref, base_ref, scale_ref, out_ref, stage, sem):
    for start, stop in zip(cuts[:-1], cuts[1:]):
        rows = pl.ds(start, stop - start)
        active = jnp.maximum(other_ref[rows, :], jnp.zeros((), jnp.bfloat16))
        part = jnp.dot(active, tap_ref[...], preferred_element_type=jnp.float32)
        stage[rows, :] = (base_ref[rows, :] + part * scale_ref[...]).astype(jnp.bfloat16)
        pltpu.make_async_copy(stage.at[rows, :], out_ref.at[rows, :], sem).start()
    pltpu.make_async_copy(stage, out_ref, sem).wait()


def finish(other, tap, base, scale):
    cells, chans = base.shape
    cuts = [cells * part // 16 for part in (0, 8, 12, 14, 15, 16)]
    whole = pl.BlockSpec(memory_space=pltpu.VMEM)
    return pl.pallas_call(
        functools.partial(finish_kernel, cuts),
        out_shape=jax.ShapeDtypeStruct(base.shape, jnp.bfloat16),
        in_specs=[whole] * 4,
        out_specs=pl.BlockSpec(memory_space=pl.ANY),
        scratch_shapes=[
            pltpu.VMEM((cells, chans), jnp.bfloat16),
            pltpu.SemaphoreType.DMA,
        ],
        compiler_params=pltpu.CompilerParams(vmem_limit_bytes=16 * MIB),
        cost_estimate=pl.CostEstimate(
            flops=2 * cells * chans * chans,
            bytes_accessed=10 * cells * chans,
            transcendentals=0,
        ),
    )(other, tap, base, scale)


def paired(encoded, conv_weight, film_table, lead, row_step):
    count = lax.axis_size("rows")
    other = lax.ppermute(encoded, "rows", [(i, (i + row_step) % count) for i in range(count)])
    above = lax.axis_index("rows") < row_step
    column = conv_weight[:, 1]
    far_tap = lax.dynamic_index_in_dim(column, jnp.where(above, 2, 0), 0, keepdims=False)
    scale, beta = film(film_table, lead)
    near = product(encoded, column[1])
    base = encoded.reshape(near.shape).astype(jnp.float32) + near * scale + beta
    updated = finish(other.reshape(near.shape), far_tap, base, scale[None])
    return updated.reshape(encoded.shape)


def local(encoded, conv_weight, film_table, lead):
    row_step = DILATION_RATE // encoded.shape[0]
    column_step = DILATION_RATE // encoded.shape[1]
    if lax.axis_size("rows") == 2 * row_step and column_step >= lax.axis_size("cols"):
        return paired(encoded, conv_weight, film_table, lead, row_step)
    return any_grid(encoded, conv_weight, film_table, lead, row_step, column_step)


def solution(mesh):
    placed = (P("rows", "cols", None), P(), P(), P())
    return jax.shard_map(
        local, mesh=mesh, in_specs=placed, out_specs=P("rows", "cols", None), check_vma=False
    )
```

```python
import functools

import jax
import jax.numpy as jnp
from jax import lax
from jax.experimental import pallas as pl
from jax.experimental.pallas import tpu as pltpu
from jax.sharding import PartitionSpec as P

DILATION_RATE = 128
MIB = 1 << 20


def shifted(block, axis, distance):
    devices = range(lax.axis_size(axis))
    route = [(i - distance, i) for i in devices if i - distance in devices]
    return lax.ppermute(block, axis, route)


def relu(block):
    return jnp.maximum(block, jnp.zeros((), block.dtype))


def product(block, tap):
    flat = relu(block).reshape(-1, block.shape[-1])
    return jnp.dot(flat, tap, preferred_element_type=jnp.float32)


def film(film_table, lead):
    chosen = lax.dynamic_index_in_dim(film_table, lead[0], 0, keepdims=False)
    chosen = chosen.astype(jnp.float32)
    return 1.0 + chosen[0], chosen[1]


def any_grid(encoded, conv_weight, film_table, lead, row_step, column_step):
    steps = (-1, 0, 1)
    total = jnp.zeros((encoded.shape[0] * encoded.shape[1], encoded.shape[2]), jnp.float32)
    for ky in steps:
        if abs(ky) * row_step >= lax.axis_size("rows"):
            continue
        strip = shifted(encoded, "rows", -ky * row_step) if ky else encoded
        for kx in steps:
            if abs(kx) * column_step >= lax.axis_size("cols"):
                continue
            block = shifted(strip, "cols", -kx * column_step) if kx else strip
            total = total + product(block, conv_weight[ky + 1, kx + 1])
    scale, beta = film(film_table, lead)
    flat = encoded.reshape(total.shape).astype(jnp.float32)
    return (flat + total * scale + beta).astype(jnp.bfloat16).reshape(encoded.shape)


def finish_kernel(cuts, other_ref, tap_ref, base_ref, scale_ref, out_ref, stage, sem):
    for start, stop in zip(cuts[:-1], cuts[1:]):
        rows = pl.ds(start, stop - start)
        active = jnp.maximum(other_ref[rows, :], jnp.zeros((), jnp.bfloat16))
        part = jnp.dot(active, tap_ref[...], preferred_element_type=jnp.float32)
        stage[rows, :] = (base_ref[rows, :] + part * scale_ref[...]).astype(jnp.bfloat16)
        pltpu.make_async_copy(stage.at[rows, :], out_ref.at[rows, :], sem).start()
    pltpu.make_async_copy(stage, out_ref, sem).wait()


def finish(other, tap, base, scale):
    cells, chans = base.shape
    cuts = [cells * part // 16 for part in (0, 2, 4, 8, 12, 14, 15, 16)]
    whole = pl.BlockSpec(memory_space=pltpu.VMEM)
    return pl.pallas_call(
        functools.partial(finish_kernel, cuts),
        out_shape=jax.ShapeDtypeStruct(base.shape, jnp.bfloat16),
        in_specs=[whole] * 4,
        out_specs=pl.BlockSpec(memory_space=pl.ANY),
        scratch_shapes=[
            pltpu.VMEM((cells, chans), jnp.bfloat16),
            pltpu.SemaphoreType.DMA,
        ],
        compiler_params=pltpu.CompilerParams(vmem_limit_bytes=16 * MIB),
        cost_estimate=pl.CostEstimate(
            flops=2 * cells * chans * chans,
            bytes_accessed=10 * cells * chans,
            transcendentals=0,
        ),
    )(other, tap, base, scale)


def paired(encoded, conv_weight, film_table, lead, row_step):
    count = lax.axis_size("rows")
    other = lax.ppermute(encoded, "rows", [(i, (i + row_step) % count) for i in range(count)])
    above = lax.axis_index("rows") < row_step
    column = conv_weight[:, 1]
    far_tap = lax.dynamic_index_in_dim(column, jnp.where(above, 2, 0), 0, keepdims=False)
    scale, beta = film(film_table, lead)
    near = product(encoded, column[1])
    base = encoded.reshape(near.shape).astype(jnp.float32) + near * scale + beta
    updated = finish(other.reshape(near.shape), far_tap, base, scale[None])
    return updated.reshape(encoded.shape)


def local(encoded, conv_weight, film_table, lead):
    row_step = DILATION_RATE // encoded.shape[0]
    column_step = DILATION_RATE // encoded.shape[1]
    if lax.axis_size("rows") == 2 * row_step and column_step >= lax.axis_size("cols"):
        return paired(encoded, conv_weight, film_table, lead, row_step)
    return any_grid(encoded, conv_weight, film_table, lead, row_step, column_step)


def solution(mesh):
    placed = (P("rows", "cols", None), P(), P(), P())
    return jax.shard_map(
        local, mesh=mesh, in_specs=placed, out_specs=P("rows", "cols", None), check_vma=False
    )
```

```python
import functools

import jax
import jax.numpy as jnp
from jax import lax
from jax.experimental import pallas as pl
from jax.experimental.pallas import tpu as pltpu
from jax.sharding import PartitionSpec as P

DILATION_RATE = 128
MIB = 1 << 20


def shifted(block, axis, distance):
    devices = range(lax.axis_size(axis))
    route = [(i - distance, i) for i in devices if i - distance in devices]
    return lax.ppermute(block, axis, route)


def relu(block):
    return jnp.maximum(block, jnp.zeros((), block.dtype))


def product(block, tap):
    flat = relu(block).reshape(-1, block.shape[-1])
    return jnp.dot(flat, tap, preferred_element_type=jnp.float32)


def film(film_table, lead):
    chosen = lax.dynamic_index_in_dim(film_table, lead[0], 0, keepdims=False)
    chosen = chosen.astype(jnp.float32)
    return 1.0 + chosen[0], chosen[1]


def any_grid(encoded, conv_weight, film_table, lead, row_step, column_step):
    steps = (-1, 0, 1)
    total = jnp.zeros((encoded.shape[0] * encoded.shape[1], encoded.shape[2]), jnp.float32)
    for ky in steps:
        if abs(ky) * row_step >= lax.axis_size("rows"):
            continue
        strip = shifted(encoded, "rows", -ky * row_step) if ky else encoded
        for kx in steps:
            if abs(kx) * column_step >= lax.axis_size("cols"):
                continue
            block = shifted(strip, "cols", -kx * column_step) if kx else strip
            total = total + product(block, conv_weight[ky + 1, kx + 1])
    scale, beta = film(film_table, lead)
    flat = encoded.reshape(total.shape).astype(jnp.float32)
    return (flat + total * scale + beta).astype(jnp.bfloat16).reshape(encoded.shape)


def finish_kernel(cuts, other_ref, tap_ref, base_ref, scale_ref, out_ref, stage, sem):
    for start, stop in zip(cuts[:-1], cuts[1:]):
        rows = pl.ds(start, stop - start)
        active = jnp.maximum(other_ref[rows, :], jnp.zeros((), jnp.bfloat16))
        part = jnp.dot(active, tap_ref[...], preferred_element_type=jnp.float32)
        stage[rows, :] = (base_ref[rows, :] + part * scale_ref[...]).astype(jnp.bfloat16)
        pltpu.make_async_copy(stage.at[rows, :], out_ref.at[rows, :], sem).start()
    pltpu.make_async_copy(stage, out_ref, sem).wait()


def finish(other, tap, base, scale):
    cells, chans = base.shape
    cuts = [cells * part // 16 for part in (0, 4, 8, 12, 15, 16)]
    whole = pl.BlockSpec(memory_space=pltpu.VMEM)
    return pl.pallas_call(
        functools.partial(finish_kernel, cuts),
        out_shape=jax.ShapeDtypeStruct(base.shape, jnp.bfloat16),
        in_specs=[whole] * 4,
        out_specs=pl.BlockSpec(memory_space=pl.ANY),
        scratch_shapes=[
            pltpu.VMEM((cells, chans), jnp.bfloat16),
            pltpu.SemaphoreType.DMA,
        ],
        compiler_params=pltpu.CompilerParams(vmem_limit_bytes=16 * MIB),
        cost_estimate=pl.CostEstimate(
            flops=2 * cells * chans * chans,
            bytes_accessed=10 * cells * chans,
            transcendentals=0,
        ),
    )(other, tap, base, scale)


def paired(encoded, conv_weight, film_table, lead, row_step):
    count = lax.axis_size("rows")
    other = lax.ppermute(encoded, "rows", [(i, (i + row_step) % count) for i in range(count)])
    above = lax.axis_index("rows") < row_step
    column = conv_weight[:, 1]
    far_tap = lax.dynamic_index_in_dim(column, jnp.where(above, 2, 0), 0, keepdims=False)
    scale, beta = film(film_table, lead)
    near = product(encoded, column[1])
    base = encoded.reshape(near.shape).astype(jnp.float32) + near * scale + beta
    updated = finish(other.reshape(near.shape), far_tap, base, scale[None])
    return updated.reshape(encoded.shape)


def local(encoded, conv_weight, film_table, lead):
    row_step = DILATION_RATE // encoded.shape[0]
    column_step = DILATION_RATE // encoded.shape[1]
    if lax.axis_size("rows") == 2 * row_step and column_step >= lax.axis_size("cols"):
        return paired(encoded, conv_weight, film_table, lead, row_step)
    return any_grid(encoded, conv_weight, film_table, lead, row_step, column_step)


def solution(mesh):
    placed = (P("rows", "cols", None), P(), P(), P())
    return jax.shard_map(
        local, mesh=mesh, in_specs=placed, out_specs=P("rows", "cols", None), check_vma=False
    )
```
